256 devices in a mesh: rep: 32 (over y, x, core), shard: 8 (over z).
Axes of the slice: x: 4, y: 4, z: 8, core: 2. Of those that a mesh axis runs over, the one named last changes fastest.
Arguments:
- grads: bfloat16 [32, 1024, 8192], P('rep', 'shard'), may hold values from -6 to 6
- errors: bfloat16 [32, 1024, 8192], P('rep', 'shard'), may hold values from -4 to 4
- q_prev: float32 [8192, 128], P('shard'), may hold values from -0.0625 to 0.0625
- moment: float32 [1024, 8192], P('shard'), may hold values from -0.12 to 0.12
- second: float32 [1024, 8192], P('shard'), may hold values from 0.0001 to 0.01
Outputs:
- errors_next: bfloat16 [32, 1024, 8192], P('rep', 'shard')
- q_next: float32 [8192, 128], P('shard')
- moment_next: float32 [1024, 8192], P('shard')
- second_next: float32 [1024, 8192], P('shard')
- update: bfloat16 [1024, 8192], P('shard')
The draws below stay inside these ranges and needn't reach their ends.
All inputs are finite; a program needn't handle non-finite values.
Results may differ from the reference program's by a relative error of at most 0.0012.
Values sent between devices are 32-bit elements; how exact they have to be, the bound alone decides.
No kernel may reach another device: no remote copies, remote signals or barrier semaphores. Data moves between devices by JAX's collectives and lax.ppermute only.
A program may use at most 128 MiB of HBM per device.

```python
import math
import jax
import jax.numpy as jnp
from jax import lax

C = 8192
RANK = 128
ADAM_STEP = 10
ROWS = 1024
REPS = 32


def levels(rng, shape, split, least, top_value):
    factor_of, own = 1.0, jax.random.fold_in(rng, 6)
    for position, parts in split:
        draws = jnp.exp(jax.random.uniform(jax.random.fold_in(own, position), (parts,), jnp.float32, least / len(split), top_value / len(split)))
        factor_of = factor_of * jnp.repeat(draws, shape[position] // parts).reshape([-1 if axis == position else 1 for axis in range(len(shape))])
    return factor_of


def scatter_about(stream_key, shape, scale, reach, pieces=(), kind=jnp.bfloat16):
    values = jax.random.normal(stream_key, shape, jnp.float32) * scale
    if len(pieces) > 0:
        values = levels(stream_key, shape, pieces, -0.22, 0.18) * values
    return jnp.clip(values, min=-reach, max=reach).astype(kind)


def setup_inputs(seed: int = 0) -> dict:
    seeds = jax.random.split(jax.random.key(seed), 6)
    grads = scatter_about(seeds[0], (REPS, ROWS, C), 1.0, 6.0, ((0, 32), (1, 8)))
    errors = scatter_about(seeds[1], (REPS, ROWS, C), 0.5, 4.0, ((0, 32), (1, 8)))
    q_prev = scatter_about(seeds[2], (C, RANK), C ** -0.5, 0.0625, ((0, 8),), jnp.float32)
    moment = scatter_about(seeds[3], (ROWS, C), 0.02, 0.12, ((0, 8),), jnp.float32)
    second = jnp.clip(jnp.exp(math.log(0.01) - 4.6051702 * jax.random.uniform(seeds[4], (ROWS, C), jnp.float32) ** levels(seeds[4], (ROWS, C), ((0, 8),), -0.2, 0.2)), 0.0001, 0.01)
    return {"grads": grads, "errors": errors, "q_prev": q_prev, "moment": moment, "second": second}


def reference(grads, errors, q_prev, moment, second):
    hi = lax.Precision.HIGHEST

    def p_term(carry, pair):
        merged = pair[0].astype(jnp.float32) + pair[1].astype(jnp.float32)
        return (carry + jnp.dot(merged, q_prev, precision=hi), None)
    p_init = jnp.zeros((grads.shape[1], q_prev.shape[1]), jnp.float32)
    p_sum, _ = lax.scan(p_term, p_init, (grads, errors))
    gram = jnp.dot(p_sum.T, p_sum, precision=hi)
    low = jnp.linalg.cholesky(gram)
    p_hat = lax.linalg.triangular_solve(low, p_sum, left_side=False, lower=True, transpose_a=True)

    def q_term(carry, pair):
        merged = pair[0].astype(jnp.float32) + pair[1].astype(jnp.float32)
        return (carry + jnp.dot(merged.T, p_hat, precision=hi), None)
    q_init = jnp.zeros(q_prev.shape, jnp.float32)
    q_sum, _ = lax.scan(q_term, q_init, (grads, errors))
    q_next = q_sum / REPS
    approx = jnp.dot(p_hat, q_next.T, precision=hi)

    def err_term(pair):
        merged = pair[0].astype(jnp.float32) + pair[1].astype(jnp.float32)
        return (merged - approx).astype(jnp.bfloat16)
    errors_next = lax.map(err_term, (grads, errors))
    moment_next = 0.9 * moment + 0.1 * approx
    second_next = 0.95 * second + 0.05 * approx * approx
    fix_one = 1.0 - 0.9 ** ADAM_STEP
    fix_two = 1.0 - 0.95 ** ADAM_STEP
    update = (moment_next / fix_one / (jnp.sqrt(second_next / fix_two) + 1e-08)).astype(jnp.bfloat16)
    return (errors_next, q_next, moment_next, second_next, update)
```

```python
import functools
import math

import jax
import jax.numpy as jnp
from jax import lax
from jax.experimental import pallas as pl
from jax.experimental.pallas import tpu as pltpu
from jax.sharding import Mesh, PartitionSpec as P

ADAM_STEP = 10
HI = lax.Precision.HIGHEST
F32 = jnp.float32
ALL = ("y", "x", "core", "z")
REPS = 32
VMEM_LIMIT = 40 * 1024 * 1024


def vmem():
    return pl.BlockSpec(memory_space=pltpu.VMEM)


def params():
    return pltpu.CompilerParams(vmem_limit_bytes=VMEM_LIMIT)


def dot_nt(a, b):
    return lax.dot_general(a, b, (((1,), (1,)), ((), ())), precision=HI, preferred_element_type=F32)


def add_half(place, grads, errors):
    rows, cols = grads.shape
    wide = cols // 8

    def body(at, g, e, out):
        out[...] = g[...].astype(F32) + e[...].astype(F32)

    half = pl.BlockSpec((rows, wide), lambda i, at: (0, (1 - at[0]) * 4 + i))
    return pl.pallas_call(
        body,
        grid_spec=pltpu.PrefetchScalarGridSpec(
            num_scalar_prefetch=1,
            grid=(4,),
            in_specs=[half, half],
            out_specs=pl.BlockSpec((rows, wide), lambda i, at: (0, i)),
        ),
        out_shape=jax.ShapeDtypeStruct((rows, cols // 2), F32),
        compiler_params=params(),
        name="add_half",
    )(place, grads, errors)


def add_pieces(place, grads, errors, came):
    rows, cols = grads.shape
    wide = cols // 8
    tall = rows // 4

    def body(at, *refs):
        for k in range(4):
            g, e, r = refs[3 * k : 3 * k + 3]
            refs[12 + k][...] = g[...].astype(F32) + e[...].astype(F32) + r[...]

    def own(k):
        return pl.BlockSpec((tall, wide), lambda i, at: (i, at[0] * 4 + (at[1] + k) % 4))

    def other(k):
        return pl.BlockSpec((tall, wide), lambda i, at: (i, (at[1] + k) % 4))

    ins, args = [], []
    for k in range(4):
        ins += [own(k), own(k), other(k)]
        args += [grads, errors, came]
    return pl.pallas_call(
        body,
        grid_spec=pltpu.PrefetchScalarGridSpec(
            num_scalar_prefetch=1,
            grid=(4,),
            in_specs=ins,
            out_specs=[pl.BlockSpec((tall, wide), lambda i, at: (i, 0))] * 4,
        ),
        out_shape=[jax.ShapeDtypeStruct((rows, wide), F32)] * 4,
        compiler_params=params(),
        name="add_pieces",
    )(place, *args)


def sum_split(place, parts):
    rows, cols = parts[0].shape
    wide = cols // 4

    def body(at, *refs):
        for k in range(4):
            block = pl.ds(pl.multiple_of(((at[2] + k) % 4) * wide, wide), wide)
            a, b, c, d = (r[:, block] for r in refs[:4])
            refs[4 + k][...] = (a + b) + (c + d)

    return pl.pallas_call(
        body,
        grid_spec=pltpu.PrefetchScalarGridSpec(
            num_scalar_prefetch=1,
            grid=(1,),
            in_specs=[vmem()] * 4,
            out_specs=[vmem()] * 4,
        ),
        out_shape=[jax.ShapeDtypeStruct((rows, wide), F32)] * 4,
        compiler_params=params(),
        name="sum_split",
    )(place, *parts)


def left_part(parts, right):
    rows, cols = parts[0].shape

    def body(a, b, c, d, q, m_out, p_out):
        m = (a[...] + b[...]) + (c[...] + d[...])
        m_out[...] = m
        p_out[...] = jnp.dot(m, q[...], precision=HI, preferred_element_type=F32)

    return pl.pallas_call(
        body,
        in_specs=[vmem()] * 5,
        out_specs=[vmem()] * 2,
        out_shape=[
            jax.ShapeDtypeStruct((rows, cols), F32),
            jax.ShapeDtypeStruct((rows, right.shape[1]), F32),
        ],
        compiler_params=params(),
        name="left_part",
    )(*parts, right)


def products(m, p):
    cols, rank = m.shape[1], p.shape[1]
    high, low = cols // 8, rank // 8

    def body(m_ref, p_ref, out):
        p_val = p_ref[...]
        t = jnp.dot(m_ref[...].T, p_val, precision=HI, preferred_element_type=F32)
        gram = jnp.dot(p_val.T, p_val, precision=HI, preferred_element_type=F32)
        out[:, :high, :] = t.reshape(8, high, rank)
        out[:, high:, :] = gram.reshape(8, low, rank)

    return pl.pallas_call(
        body,
        in_specs=[vmem()] * 2,
        out_specs=vmem(),
        out_shape=jax.ShapeDtypeStruct((8, high + low, rank), F32),
        compiler_params=params(),
        name="products",
    )(m, p)


def finish(place, which, t, weight, grads, errors, moment, second, before):
    rows, cols = grads.shape
    rank = t.shape[1]
    wide = t.shape[0] // 4
    fix_one = 1.0 / (1.0 - 0.9**ADAM_STEP)
    fix_two = 1.0 / (1.0 - 0.95**ADAM_STEP)
    kc, kx = which

    def body(at, t_ref, w_ref, g, e, m, v, *refs):
        e_out, m_out, v_out, u_out = refs[-4:]
        approx = dot_nt(w_ref[...], t_ref[...])
        merged = g[...].astype(F32) + e[...].astype(F32)
        e_out[...] = (merged - approx).astype(jnp.bfloat16)
        m_next = 0.9 * m[...] + 0.1 * approx
        v_next = 0.95 * v[...] + 0.05 * approx * approx
        m_out[...] = m_next
        v_out[...] = v_next
        u_out[...] = (m_next * fix_one / (jnp.sqrt(v_next * fix_two) + 1e-08)).astype(jnp.bfloat16)

    def column(i, at):
        core = at[0] if kc == 0 else 1 - at[0]
        return (0, (core * 4 + (at[1] + 4 - kx) % 4) * 4 + (at[2] + 4 - i) % 4)

    block = pl.BlockSpec((rows, wide), column)
    ins = [
        pl.BlockSpec((wide, rank), lambda i, at: (i, 0)),
        pl.BlockSpec((rows, rank), lambda i, at: (0, 0)),
        block,
        block,
        block,
        block,
    ]
    args = [place, t, weight, grads, errors, moment, second]
    alias = {}
    if before is not None:
        ins += [pl.BlockSpec(memory_space=pl.ANY)] * 4
        alias = {len(args) + i: i for i in range(4)}
        args += list(before)
    return pl.pallas_call(
        body,
        grid_spec=pltpu.PrefetchScalarGridSpec(
            num_scalar_prefetch=1, grid=(4,), in_specs=ins, out_specs=[block] * 4
        ),
        out_shape=[
            jax.ShapeDtypeStruct((rows, cols), d) for d in (jnp.bfloat16, F32, F32, jnp.bfloat16)
        ],
        input_output_aliases=alias,
        compiler_params=params(),
        name="finish",
    )(*args)


def shift(value, axis, step):
    n = lax.axis_size(axis)
    return lax.ppermute(value, axis, [(i, (i + step) % n) for i in range(n)])


def device(y, x, core, z):
    return ((y * 4 + x) * 2 + core) * 8 + z


def spread(block, steps, held):
    pairs = []
    for y in range(4):
        for x in range(4):
            for core in range(2):
                for h in held:
                    z = (core * 4 + x + h) % 8
                    pairs.append((device(y, x, core, z), device(y, x, core, (z + steps) % 8)))
    return lax.ppermute(block, ALL, pairs)


def on_device(grads, errors, q_prev, moment, second):
    y, x, core, z = (lax.axis_index(a) for a in ALL)
    place = jnp.stack([core, x, y, z]).astype(jnp.int32)
    grads, errors = grads[0], errors[0]

    width = q_prev.shape[0] // 4
    away = (z - (core * 4 + x)) % 8
    right = lax.dynamic_slice_in_dim(q_prev, y * width, width, 0)
    held = [0]
    for step in (4, 2, 1):
        came = spread(right, step, held)
        new = [h + step for h in held]
        hit = functools.reduce(jnp.logical_or, [away == h for h in new])
        right = jnp.where(hit, came, right)
        held = held + new

    came = shift(add_half(place, grads, errors), "core", 1)
    pieces = add_pieces(place, grads, errors, came)
    pieces = [pieces[0]] + [shift(pieces[k], "x", k) for k in (1, 2, 3)]
    pieces = sum_split(place, pieces)
    pieces = [pieces[0]] + [shift(pieces[k], "y", k) for k in (1, 2, 3)]
    m, p = left_part(pieces, right)

    for axis in ("x", "y"):
        p = (p + shift(p, axis, 1)) + (shift(p, axis, 2) + shift(p, axis, 3))
    p = p + shift(p, "core", 1)

    mine = lax.all_to_all(products(m, p), "z", 0, 0)
    mine = jnp.sum(mine, axis=0)
    whole = lax.all_to_all(jnp.broadcast_to(mine, (8,) + mine.shape), "z", 0, 0)
    high = m.shape[1] // 8
    rank = p.shape[1]
    t = whole[:, :high].reshape(m.shape[1], rank)
    gram = whole[:, high:].reshape(rank, rank)

    t = jnp.concatenate([t] + [shift(t, "y", k) for k in (1, 2, 3)], axis=0)
    ts = [t] + [shift(t, "x", k) for k in (1, 2, 3)]

    low = jnp.linalg.cholesky(gram)
    inverse = lax.linalg.triangular_solve(low, jnp.eye(rank, dtype=F32), left_side=True, lower=True)
    p_hat = jnp.dot(p, inverse.T, precision=HI)
    weight = jnp.dot(p_hat, inverse, precision=HI) * (1.0 / REPS)

    out = None
    mine = jnp.zeros_like(t)
    for k in range(4):
        for c, piece in enumerate((ts[k], shift(ts[k], "core", 1))):
            out = finish(place, (c, k), piece, weight, grads, errors, moment, second, out)
            owner = (core ^ c) * 4 + (x + 4 - k) % 4
            mine = jnp.where(owner == z, piece, mine)
    mine = jnp.dot(mine, inverse.T, precision=HI) * (1.0 / REPS)
    mine = mine.reshape(4, width, rank)
    q_next = jnp.concatenate(
        [lax.dynamic_slice_in_dim(mine, (y - j) % 4, 1, 0)[0] for j in range(4)], axis=0
    )
    e_next, m_next, v_next, update = out
    return (e_next[None], q_next, m_next, v_next, update)


def solution(mesh):
    grid = Mesh(mesh.devices.reshape(4, 4, 2, 8), ALL)
    rep = ("y", "x", "core")
    return jax.shard_map(
        on_device,
        mesh=grid,
        in_specs=(P(rep, "z", None), P(rep, "z", None), P("z", None), P("z", None), P("z", None)),
        out_specs=(P(rep, "z", None), P("z", None), P("z", None), P("z", None), P("z", None)),
        check_vma=False,
    )
```

```python
import functools

import jax
import jax.numpy as jnp
from jax import lax
from jax.experimental import pallas as pl
from jax.experimental.pallas import tpu as pltpu
from jax.sharding import Mesh, PartitionSpec as P

ADAM_STEP = 10
HI = lax.Precision.HIGHEST
F32 = jnp.float32
ALL = ("y", "x", "core", "z")
REPS = 32


def vmem():
    return pl.BlockSpec(memory_space=pltpu.VMEM)


def params(mib=16):
    return pltpu.CompilerParams(vmem_limit_bytes=mib * 1024 * 1024)


def dot_nt(a, b):
    return lax.dot_general(a, b, (((1,), (1,)), ((), ())), precision=HI, preferred_element_type=F32)


def merge_half(place, other, grads, errors):
    rows, cols = grads.shape
    wide = cols // 8
    thin = wide // 4
    tall = rows // 2

    def body(at, g, e, *outs):
        core = 1 - at[0] if other else at[0]
        for k in range(4):
            for j in range(4):
                for side in range(2):
                    x, y = (j, k) if side else (k, j)
                    block = core * 16 + (at[1] + x) % 4 * 4 + (at[2] + y) % 4
                    block = pl.ds(pl.multiple_of(block * thin, thin), thin)
                    part = slice(side * tall, (side + 1) * tall)
                    outs[k][part, j * thin : (j + 1) * thin] = g[part, block].astype(F32) + e[
                        part, block
                    ].astype(F32)

    return pl.pallas_call(
        body,
        in_specs=[pl.BlockSpec(memory_space=pltpu.SMEM)] + [vmem()] * 2,
        out_specs=[vmem()] * 4,
        out_shape=[jax.ShapeDtypeStruct((rows, wide), F32)] * 4,
        compiler_params=params(),
        name="merge_half",
    )(place, grads, errors)


def add_two(own, came):
    rows, wide = own.shape
    tall = rows // 2

    def body(a, b, up, down):
        up[...] = a[:tall] + b[:tall]
        down[...] = a[tall:] + b[tall:]

    return pl.pallas_call(
        body,
        in_specs=[vmem()] * 2,
        out_specs=[vmem()] * 2,
        out_shape=[jax.ShapeDtypeStruct((tall, wide), F32)] * 2,
        compiler_params=params(),
        name="add_two",
    )(own, came)


def sum_split(own, came, ups, downs):
    rows, wide = own.shape
    tall, thin = rows // 2, wide // 4

    def body(a, b, *refs):
        outs = refs[6:]
        for k in range(4):
            block = slice(k * thin, (k + 1) * thin)
            for side in range(2):
                part = slice(side * tall, (side + 1) * tall)
                c, d, e = (r[:, block] for r in refs[3 * side : 3 * side + 3])
                outs[4 * side + k][...] = (a[part, block] + b[part, block]) + (c + d) + e

    return pl.pallas_call(
        body,
        in_specs=[vmem()] * 8,
        out_specs=[vmem()] * 8,
        out_shape=[jax.ShapeDtypeStruct((tall, thin), F32)] * 8,
        compiler_params=params(),
        name="sum_split",
    )(own, came, *ups, *downs)


def left_part(ups, downs, right):
    tall, cols = ups[0].shape

    def body(*refs):
        q, m_out, p_out = refs[8:]
        for side in range(2):
            a, b, c, d = (r[...] for r in refs[4 * side : 4 * side + 4])
            m_out[side * tall : (side + 1) * tall, :] = (a + b) + (c + d)
        p_out[...] = jnp.dot(m_out[...], q[...], precision=HI, preferred_element_type=F32)

    return pl.pallas_call(
        body,
        in_specs=[vmem()] * 9,
        out_specs=[vmem()] * 2,
        out_shape=[
            jax.ShapeDtypeStruct((2 * tall, cols), F32),
            jax.ShapeDtypeStruct((2 * tall, right.shape[1]), F32),
        ],
        compiler_params=params(),
        name="left_part",
    )(*ups, *downs, right)


def products(m, p):
    cols, rank = m.shape[1], p.shape[1]
    high, low = cols // 8, rank // 8

    def body(m_ref, p_ref, out):
        p_val = p_ref[...]
        t = jnp.dot(m_ref[...].T, p_val, precision=HI, preferred_element_type=F32)
        gram = jnp.dot(p_val.T, p_val, precision=HI, preferred_element_type=F32)
        out[:, :high, :] = t.reshape(8, high, rank)
        out[:, high:, :] = gram.reshape(8, low, rank)

    return pl.pallas_call(
        body,
        in_specs=[vmem()] * 2,
        out_specs=vmem(),
        out_shape=jax.ShapeDtypeStruct((8, high + low, rank), F32),
        compiler_params=params(),
        name="products",
    )(m, p)


def total(parts):
    def body(*refs):
        value = refs[0][...]
        for ref in refs[1:-1]:
            value = value + ref[...]
        refs[-1][...] = value

    return pl.pallas_call(
        body,
        in_specs=[vmem()] * len(parts),
        out_specs=vmem(),
        out_shape=jax.ShapeDtypeStruct(parts[0].shape, F32),
        compiler_params=params(),
        name="total",
    )(*parts)


def stack(parts):
    rows, cols = parts[0].shape

    def body(*refs):
        for i in range(len(parts)):
            refs[-1][i * rows : (i + 1) * rows, :] = refs[i][...]

    return pl.pallas_call(
        body,
        in_specs=[vmem()] * len(parts),
        out_specs=vmem(),
        out_shape=jax.ShapeDtypeStruct((len(parts) * rows, cols), F32),
        compiler_params=params(),
        name="stack",
    )(*parts)


def halves(a, b):
    rows, cols = a.shape[0] // 2, a.shape[1]

    def body(a_ref, b_ref, up, down):
        up[...] = a_ref[:rows]
        down[...] = b_ref[rows:]

    return pl.pallas_call(
        body,
        in_specs=[vmem()] * 2,
        out_specs=[vmem()] * 2,
        out_shape=[jax.ShapeDtypeStruct((rows, cols), F32)] * 2,
        compiler_params=params(),
        name="halves",
    )(a, b)


def sum_copies(parts):
    def body(a, out):
        value = jnp.sum(a[...], axis=0)
        out[...] = jnp.broadcast_to(value[None], out.shape)

    return pl.pallas_call(
        body,
        in_specs=[vmem()],
        out_specs=vmem(),
        out_shape=jax.ShapeDtypeStruct(parts.shape, F32),
        compiler_params=params(),
        name="sum_copies",
    )(parts)


def unpack(whole, high):
    count, both, rank = whole.shape
    low = both - high

    def body(a, t, gram):
        for i in range(count):
            t[i * high : (i + 1) * high, :] = a[i, :high, :]
            gram[i * low : (i + 1) * low, :] = a[i, high:, :]

    return pl.pallas_call(
        body,
        in_specs=[vmem()],
        out_specs=[vmem()] * 2,
        out_shape=[
            jax.ShapeDtypeStruct((count * high, rank), F32),
            jax.ShapeDtypeStruct((count * low, rank), F32),
        ],
        compiler_params=params(),
        name="unpack",
    )(whole)


def rows_of(place, q_prev):
    rows = q_prev.shape[0] // 4

    def body(at, q, out):
        out[...] = q[pl.ds(pl.multiple_of(at[2] * rows, rows), rows), :]

    return pl.pallas_call(
        body,
        in_specs=[pl.BlockSpec(memory_space=pltpu.SMEM), vmem()],
        out_specs=vmem(),
        out_shape=jax.ShapeDtypeStruct((rows, q_prev.shape[1]), F32),
        compiler_params=params(),
        name="rows_of",
    )(place, q_prev)


def choose(place, hits, came, have):
    def body(at, a, b, out):
        away = (at[3] + 8 - (at[0] * 4 + at[1])) % 8
        hit = functools.reduce(jnp.logical_or, [away == h for h in hits])
        out[...] = jnp.where(hit, a[...], b[...])

    return pl.pallas_call(
        body,
        in_specs=[pl.BlockSpec(memory_space=pltpu.SMEM)] + [vmem()] * 2,
        out_specs=vmem(),
        out_shape=jax.ShapeDtypeStruct(came.shape, F32),
        compiler_params=params(),
        name="choose",
    )(place, came, have)


ORDER = (0, 1, 3, 2)
UNIT = 8
STRIP = 16


def invert(gram, p):
    n = gram.shape[0]

    def unit(left, right, at):
        wide = (1, 2 * n)

        def element(i, j):
            return jnp.broadcast_to(left[i : i + 1, at + j : at + j + 1], wide)

        a = [[element(i, j) for j in range(i + 1)] for i in range(UNIT)]
        rows = [
            jnp.concatenate([left[i : i + 1, :], right[i : i + 1, :]], axis=1) for i in range(UNIT)
        ]
        for j in range(UNIT):
            scale = lax.rsqrt(a[j][j])
            rows[j] = rows[j] * scale
            col = [a[i][j] * scale for i in range(j + 1, UNIT)]
            for i in range(j + 1, UNIT):
                for k in range(j + 1, i + 1):
                    a[i][k] = a[i][k] - col[i - j - 1] * col[k - j - 1]
                rows[i] = rows[i] - col[i - j - 1] * rows[j]
        both = jnp.concatenate(rows, axis=0)
        return both[:, :n], both[:, n:]

    def body(g_ref, p_ref, inv_out, w_out, work):
        row = lax.broadcasted_iota(jnp.int32, (n, n), 0)
        col = lax.broadcasted_iota(jnp.int32, (n, n), 1)
        work[:, :n] = g_ref[...]
        work[:, n:] = jnp.where(row == col, 1.0, 0.0).astype(F32)
        for at in range(0, n, STRIP):
            mid, end = at + UNIT, at + STRIP
            left, right = unit(work[at:mid, :n], work[at:mid, n:], at)
            low_left, low_right = work[mid:end, :n], work[mid:end, n:]
            factors = left[:, mid:end].T
            for j in range(UNIT):
                factor = factors[:, j : j + 1]
                low_left = low_left - factor * left[j : j + 1, :]
                low_right = low_right - factor * right[j : j + 1, :]
            low_left, low_right = unit(low_left, low_right, mid)
            inv_out[at:mid, :] = right
            inv_out[mid:end, :] = low_right
            if end < n:
                strip = jnp.concatenate([left, low_left], axis=0)
                both = jnp.concatenate(
                    [strip, jnp.concatenate([right, low_right], axis=0)], axis=1
                )
                work[end:, :] -= lax.dot_general(
                    strip[:, end:],
                    both,
                    (((0,), (0,)), ((), ())),
                    precision=HI,
                    preferred_element_type=F32,
                )
        inv = inv_out[...]
        p_hat = dot_nt(p_ref[...], inv)
        w_out[...] = jnp.dot(p_hat, inv, precision=HI, preferred_element_type=F32) * (1.0 / REPS)

    return pl.pallas_call(
        body,
        in_specs=[vmem()] * 2,
        out_specs=[vmem()] * 2,
        out_shape=[jax.ShapeDtypeStruct((n, n), F32), jax.ShapeDtypeStruct(p.shape, F32)],
        scratch_shapes=[pltpu.VMEM((n, 2 * n), F32)],
        compiler_params=params(),
        cost_estimate=pl.CostEstimate(flops=8 * 10**9, bytes_accessed=1 << 18, transcendentals=n),
        name="invert",
    )(gram, p)


def finish(place, which, ts, weight, merged, moment, second, before=(), extra=()):
    rows, cols = moment.shape
    tall = rows // 2
    count = len(ts)
    wide, rank = ts[0].shape
    thin = wide // 4
    fix_one = 1.0 / (1.0 - 0.9**ADAM_STEP)
    fix_two = 1.0 / (1.0 - 0.95**ADAM_STEP)
    tail = len(before) + len(extra)

    def body(at, *refs):
        blocks = refs[count : count + 8]
        w_ref, m, v = refs[count + 8 : count + 11]
        outs = refs[count + 11 + tail :]
        e_out, m_out, v_out, u_out = outs[:4]
        for i in range(count):

            @pl.when(pl.program_id(0) == i)
            def _(i=i):
                kc, kx = i % 2, (4 - i // 2 - which) % 4
                for j in range(4):
                    ky = (4 - j) % 4
                    block = pl.ds(pl.multiple_of(((at[2] + ky) % 4) * thin, thin), thin)
                    t = refs[i][j * thin : (j + 1) * thin, :]
                    approx = dot_nt(w_ref[...], t)
                    up = blocks[4 * kc + kx][:tall, ky * thin : (ky + 1) * thin]
                    down = blocks[4 * kc + ky][tall:, kx * thin : (kx + 1) * thin]
                    e_out[:tall, block] = (up - approx[:tall]).astype(jnp.bfloat16)
                    e_out[tall:, block] = (down - approx[tall:]).astype(jnp.bfloat16)
                    m_next = 0.9 * m[:, block] + 0.1 * approx
                    v_next = 0.95 * v[:, block] + 0.05 * approx * approx
                    m_out[:, block] = m_next
                    v_out[:, block] = v_next
                    root = v_next * fix_two
                    root = root * lax.rsqrt(root)
                    u_out[:, block] = ((m_next * fix_one) / (root + 1e-08)).astype(jnp.bfloat16)

        if extra:
            inv = refs[count + 11 + tail - 1]
            near = refs[count + 11 + 4 : count + 11 + tail - 1]
            for i, t in enumerate((*near, *refs[:count])):
                core = at[0] if i % 2 == 0 else 1 - at[0]
                owner = core * 4 + (at[1] + 4 - ORDER[i // 2]) % 4

                @pl.when(jnp.logical_and(pl.program_id(0) == 0, owner == at[3]))
                def _(t=t):
                    for j in range(4):
                        part = pl.ds(pl.multiple_of(((at[2] + 4 - j) % 4) * thin, thin), thin)
                        value = dot_nt(t[j * thin : (j + 1) * thin, :], inv[...])
                        outs[4][part, :] = value * (1.0 / REPS)

    def column(i, at):
        kc, kx = i % 2, i // 2 + which
        core = at[0] + kc - 2 * at[0] * kc
        return (0, core * 4 + (at[1] + 4 - kx) % 4)

    block = pl.BlockSpec((rows, wide), column)
    ins = [vmem()] * (count + 9) + [block] * 2
    args = [place, *ts, *merged, weight, moment, second]
    specs = [block] * 4
    shapes = [
        jax.ShapeDtypeStruct((rows, cols), d) for d in (jnp.bfloat16, F32, F32, jnp.bfloat16)
    ]
    alias = {len(args) + i: i for i in range(len(before))}
    ins += [pl.BlockSpec(memory_space=pl.ANY)] * len(before) + [vmem()] * len(extra)
    args += [*before, *extra]
    if extra:
        specs.append(vmem())
        shapes.append(jax.ShapeDtypeStruct((wide, rank), F32))
    return pl.pallas_call(
        body,
        grid_spec=pltpu.PrefetchScalarGridSpec(
            num_scalar_prefetch=1, grid=(count,), in_specs=ins, out_specs=specs
        ),
        out_shape=shapes,
        input_output_aliases=alias,
        compiler_params=params(28),
        name="finish",
    )(*args)


def shift(value, axis, step):
    n = lax.axis_size(axis)
    return lax.ppermute(value, axis, [(i, (i + step) % n) for i in range(n)])


def device(y, x, core, z):
    return ((y * 4 + x) * 2 + core) * 8 + z


def spread(block, steps, held):
    pairs = []
    for y in range(4):
        for x in range(4):
            for core in range(2):
                for h in held:
                    z = (core * 4 + x + h) % 8
                    pairs.append((device(y, x, core, z), device(y, x, core, (z + steps) % 8)))
    return lax.ppermute(block, ALL, pairs)


def on_device(grads, errors, q_prev, moment, second):
    y, x, core, z = (lax.axis_index(a) for a in ALL)
    place = jnp.stack([core, x, y, z]).astype(jnp.int32)
    grads, errors = grads[0], errors[0]

    theirs = merge_half(place, True, grads, errors)
    came = {k: shift(theirs[k], "core", 1) for k in (1, 2, 3, 0)}
    mine = merge_half(place, False, grads, errors)
    merged = [*mine, *theirs]

    right = rows_of(place, q_prev)
    held = [0]
    for step in (4, 2, 1):
        new = [h + step for h in held]
        right = choose(place, new, spread(right, step, held), right)
        held = held + new

    ups, downs = [], []
    for k in (1, 2, 3):
        up, down = add_two(mine[k], came[k])
        ups.append(shift(up, "x", k))
        downs.append(shift(down, "y", k))
    blocks = sum_split(mine[0], came[0], ups, downs)
    ups = [blocks[0]] + [shift(blocks[k], "y", k) for k in (1, 2, 3)]
    downs = [blocks[4]] + [shift(blocks[4 + k], "x", k) for k in (1, 2, 3)]
    m, p = left_part(ups, downs, right)

    for axis in ("x", "y"):
        p = total([p] + [shift(p, axis, k) for k in (1, 2, 3)])
    p = total([p, shift(p, "core", 1)])

    whole = lax.all_to_all(products(m, p), "z", 0, 0)
    whole = lax.all_to_all(sum_copies(whole), "z", 0, 0)
    t, gram = unpack(whole, m.shape[1] // 8)
    t = stack([t] + [shift(t, "y", k) for k in (1, 2, 3)])
    t, gram = lax.optimization_barrier((t, gram))
    def pair(block):
        return [block, shift(block, "core", 1)]

    near = pair(t)
    one, three = shift(t, "x", 1), shift(t, "x", 3)
    inverse, weight = invert(gram, p)
    out = finish(place, 0, near, weight, merged, moment, second)
    out, one, three = lax.optimization_barrier((out, one, three))

    upper, lower = halves(one, three)
    two = [shift(upper, "x", 1), shift(lower, "x", 3)]
    one, three = pair(one), pair(three)
    out = finish(place, 1, one, weight, merged, moment, second, out)
    out = finish(place, 3, three, weight, merged, moment, second, out)
    out, two = lax.optimization_barrier((out, two))
    two = pair(stack(two))
    e_next, m_next, v_next, update, q_next = finish(
        place, 2, two, weight, merged, moment, second, out, [*near, *one, *three, inverse]
    )
    return (e_next[None], q_next, m_next, v_next, update)


def solution(mesh):
    grid = Mesh(mesh.devices.reshape(4, 4, 2, 8), ALL)
    rep = ("y", "x", "core")
    return jax.shard_map(
        on_device,
        mesh=grid,
        in_specs=(P(rep, "z", None), P(rep, "z", None), P("z", None), P("z", None), P("z", None)),
        out_specs=(P(rep, "z", None), P("z", None), P("z", None), P("z", None), P("z", None)),
        check_vma=False,
    )
```

```python
import functools

import jax
import jax.numpy as jnp
from jax import lax
from jax.experimental import pallas as pl
from jax.experimental.pallas import tpu as pltpu
from jax.sharding import Mesh, PartitionSpec as P

ADAM_STEP = 10
HI = lax.Precision.HIGHEST
F32 = jnp.float32
ALL = ("y", "x", "core", "z")
REPS = 32


def vmem():
    return pl.BlockSpec(memory_space=pltpu.VMEM)


def params(mib=16):
    return pltpu.CompilerParams(vmem_limit_bytes=mib * 1024 * 1024)


def split(value):
    high = value.astype(jnp.bfloat16)
    rest = value - high.astype(F32)
    middle = rest.astype(jnp.bfloat16)
    return high, middle, (rest - middle.astype(F32)).astype(jnp.bfloat16)


def short_nt(a, b):
    return lax.dot_general(a, b, (((1,), (1,)), ((), ())), preferred_element_type=F32)


def dot_nt(a, b):
    return lax.dot_general(a, b, (((1,), (1,)), ((), ())), precision=HI, preferred_element_type=F32)


def merge_half(place, other, grads, errors):
    rows, cols = grads.shape
    wide = cols // 8
    thin = wide // 4

    def body(at, g, e, *outs):
        core = 1 - at[0] if other else at[0]
        for k in range(4):
            for j in range(4):
                block = core * 16 + (at[1] + k) % 4 * 4 + (at[2] + j) % 4
                block = pl.ds(pl.multiple_of(block * thin, thin), thin)
                value = g[:, block].astype(F32) + e[:, block].astype(F32)
                outs[k][:, j * thin : (j + 1) * thin] = value

    return pl.pallas_call(
        body,
        in_specs=[pl.BlockSpec(memory_space=pltpu.SMEM)] + [vmem()] * 2,
        out_specs=[vmem()] * 4,
        out_shape=[jax.ShapeDtypeStruct((rows, wide), F32)] * 4,
        compiler_params=params(),
        name="merge_half",
    )(place, grads, errors)


def sum_split(parts):
    rows, wide = parts[0].shape
    thin = wide // 4
    count = len(parts)

    def body(*refs):
        for k in range(4):
            value = refs[0][:, k * thin : (k + 1) * thin]
            for ref in refs[1:count]:
                value = value + ref[:, k * thin : (k + 1) * thin]
            refs[count + k][...] = value

    return pl.pallas_call(
        body,
        in_specs=[vmem()] * count,
        out_specs=[vmem()] * 4,
        out_shape=[jax.ShapeDtypeStruct((rows, thin), F32)] * 4,
        compiler_params=params(),
        name="sum_split",
    )(*parts)


def left_part(parts, right):
    rows, cols = parts[0].shape

    def body(a, b, c, d, q, m_out, p_out):
        m_out[...] = (a[...] + b[...]) + (c[...] + d[...])
        p_out[...] = jnp.dot(m_out[...], q[...], precision=HI, preferred_element_type=F32)

    return pl.pallas_call(
        body,
        in_specs=[vmem()] * 5,
        out_specs=[vmem()] * 2,
        out_shape=[
            jax.ShapeDtypeStruct((rows, cols), F32),
            jax.ShapeDtypeStruct((rows, right.shape[1]), F32),
        ],
        compiler_params=params(),
        name="left_part",
    )(*parts, right)


def products(m, p):
    cols, rank = m.shape[1], p.shape[1]
    high, low = cols // 8, rank // 8

    def body(m_ref, p_ref, out):
        p_val = p_ref[...]
        t = jnp.dot(m_ref[...].T, p_val, precision=HI, preferred_element_type=F32)
        gram = jnp.dot(p_val.T, p_val, precision=HI, preferred_element_type=F32)
        out[:, :high, :] = t.reshape(8, high, rank)
        out[:, high:, :] = gram.reshape(8, low, rank)

    return pl.pallas_call(
        body,
        in_specs=[vmem()] * 2,
        out_specs=vmem(),
        out_shape=jax.ShapeDtypeStruct((8, high + low, rank), F32),
        compiler_params=params(),
        name="products",
    )(m, p)


def total(parts):
    def body(*refs):
        value = refs[0][...]
        for ref in refs[1:-1]:
            value = value + ref[...]
        refs[-1][...] = value

    return pl.pallas_call(
        body,
        in_specs=[vmem()] * len(parts),
        out_specs=vmem(),
        out_shape=jax.ShapeDtypeStruct(parts[0].shape, F32),
        compiler_params=params(),
        name="total",
    )(*parts)


def stack(parts):
    rows, cols = parts[0].shape

    def body(*refs):
        for i in range(len(parts)):
            refs[-1][i * rows : (i + 1) * rows, :] = refs[i][...]

    return pl.pallas_call(
        body,
        in_specs=[vmem()] * len(parts),
        out_specs=vmem(),
        out_shape=jax.ShapeDtypeStruct((len(parts) * rows, cols), F32),
        compiler_params=params(),
        name="stack",
    )(*parts)


def halves(a, b):
    rows, cols = a.shape[0] // 2, a.shape[1]

    def body(a_ref, b_ref, up, down):
        up[...] = a_ref[:rows]
        down[...] = b_ref[rows:]

    return pl.pallas_call(
        body,
        in_specs=[vmem()] * 2,
        out_specs=[vmem()] * 2,
        out_shape=[jax.ShapeDtypeStruct((rows, cols), F32)] * 2,
        compiler_params=params(),
        name="halves",
    )(a, b)


def sum_copies(parts):
    def body(a, out):
        value = jnp.sum(a[...], axis=0)
        out[...] = jnp.broadcast_to(value[None], out.shape)

    return pl.pallas_call(
        body,
        in_specs=[vmem()],
        out_specs=vmem(),
        out_shape=jax.ShapeDtypeStruct(parts.shape, F32),
        compiler_params=params(),
        name="sum_copies",
    )(parts)


def unpack(whole, high):
    count, both, rank = whole.shape
    low = both - high

    def body(a, t, gram):
        for i in range(count):
            t[i * high : (i + 1) * high, :] = a[i, :high, :]
            gram[i * low : (i + 1) * low, :] = a[i, high:, :]

    return pl.pallas_call(
        body,
        in_specs=[vmem()],
        out_specs=[vmem()] * 2,
        out_shape=[
            jax.ShapeDtypeStruct((count * high, rank), F32),
            jax.ShapeDtypeStruct((count * low, rank), F32),
        ],
        compiler_params=params(),
        name="unpack",
    )(whole)


def rows_of(place, q_prev):
    rows = q_prev.shape[0] // 4

    def body(at, q, out):
        out[...] = q[pl.ds(pl.multiple_of(at[2] * rows, rows), rows), :]

    return pl.pallas_call(
        body,
        in_specs=[pl.BlockSpec(memory_space=pltpu.SMEM), vmem()],
        out_specs=vmem(),
        out_shape=jax.ShapeDtypeStruct((rows, q_prev.shape[1]), F32),
        compiler_params=params(),
        name="rows_of",
    )(place, q_prev)


def choose(place, hits, came, have):
    def body(at, a, b, out):
        away = (at[3] + 8 - (at[0] * 4 + at[1])) % 8
        hit = functools.reduce(jnp.logical_or, [away == h for h in hits])
        out[...] = jnp.where(hit, a[...], b[...])

    return pl.pallas_call(
        body,
        in_specs=[pl.BlockSpec(memory_space=pltpu.SMEM)] + [vmem()] * 2,
        out_specs=vmem(),
        out_shape=jax.ShapeDtypeStruct(came.shape, F32),
        compiler_params=params(),
        name="choose",
    )(place, came, have)


ORDER = (0, 1, 3, 2)
UNIT = 8
STRIP = 16


def invert(gram, p):
    n = gram.shape[0]

    def unit(left, right, at):
        wide = (1, 2 * n)

        def element(i, j):
            return jnp.broadcast_to(left[i : i + 1, at + j : at + j + 1], wide)

        a = [[element(i, j) for j in range(i + 1)] for i in range(UNIT)]
        rows = [
            jnp.concatenate([left[i : i + 1, :], right[i : i + 1, :]], axis=1) for i in range(UNIT)
        ]
        for j in range(UNIT):
            scale = lax.rsqrt(a[j][j])
            rows[j] = rows[j] * scale
            col = [a[i][j] * scale for i in range(j + 1, UNIT)]
            for i in range(j + 1, UNIT):
                for k in range(j + 1, i + 1):
                    a[i][k] = a[i][k] - col[i - j - 1] * col[k - j - 1]
                rows[i] = rows[i] - col[i - j - 1] * rows[j]
        both = jnp.concatenate(rows, axis=0)
        return both[:, :n], both[:, n:]

    def body(g_ref, p_ref, inv_out, w_out, work):
        row = lax.broadcasted_iota(jnp.int32, (n, n), 0)
        col = lax.broadcasted_iota(jnp.int32, (n, n), 1)
        work[:, :n] = g_ref[...]
        work[:, n:] = jnp.where(row == col, 1.0, 0.0).astype(F32)
        for at in range(0, n, STRIP):
            mid, end = at + UNIT, at + STRIP
            left, right = unit(work[at:mid, :n], work[at:mid, n:], at)
            low_left, low_right = work[mid:end, :n], work[mid:end, n:]
            factors = left[:, mid:end].T
            for j in range(UNIT):
                factor = factors[:, j : j + 1]
                low_left = low_left - factor * left[j : j + 1, :]
                low_right = low_right - factor * right[j : j + 1, :]
            low_left, low_right = unit(low_left, low_right, mid)
            inv_out[at:mid, :] = right
            inv_out[mid:end, :] = low_right
            if end < n:
                strip = jnp.concatenate([left, low_left], axis=0)
                both = jnp.concatenate(
                    [strip, jnp.concatenate([right, low_right], axis=0)], axis=1
                )
                work[end:, :] -= lax.dot_general(
                    strip[:, end:],
                    both,
                    (((0,), (0,)), ((), ())),
                    precision=HI,
                    preferred_element_type=F32,
                )
        inv = inv_out[...]
        p_hat = dot_nt(p_ref[...], inv)
        weight = jnp.dot(p_hat, inv, precision=HI, preferred_element_type=F32) * (1.0 / REPS)
        high, middle, low = split(weight)
        for i, pair in enumerate(((high, high), (middle, middle), (low, high))):
            w_out[i * n : (i + 1) * n, :] = jnp.concatenate(pair, axis=1)

    return pl.pallas_call(
        body,
        in_specs=[vmem()] * 2,
        out_specs=[vmem()] * 2,
        out_shape=[jax.ShapeDtypeStruct((n, n), F32), jax.ShapeDtypeStruct((3 * n, 2 * n), jnp.bfloat16)],
        scratch_shapes=[pltpu.VMEM((n, 2 * n), F32)],
        compiler_params=params(),
        cost_estimate=pl.CostEstimate(flops=8 * 10**9, bytes_accessed=1 << 18, transcendentals=n),
        name="invert",
    )(gram, p)


def finish(place, which, ts, weight, merged, moment, second, before=(), extra=()):
    rows, cols = moment.shape
    count = len(ts)
    wide, rank = ts[0].shape
    thin = wide // 4
    fix_one = 1.0 / (1.0 - 0.9**ADAM_STEP)
    fix_two = 1.0 / (1.0 - 0.95**ADAM_STEP)
    tail = len(before) + len(extra)

    def body(at, *refs):
        blocks = refs[count : count + 8]
        w_ref, m, v = refs[count + 8 : count + 11]
        outs = refs[count + 11 + tail :]
        e_out, m_out, v_out, u_out = outs[:4]
        for i in range(count):

            @pl.when(pl.program_id(0) == i)
            def _(i=i):
                kc, kx = i % 2, (4 - i // 2 - which) % 4
                for j in range(4):
                    ky = (4 - j) % 4
                    block = pl.ds(pl.multiple_of(((at[2] + ky) % 4) * thin, thin), thin)
                    t = refs[i][j * thin : (j + 1) * thin, :]
                    high, middle, low = split(t)
                    big = short_nt(w_ref[: 2 * rows, :], jnp.concatenate([high, middle], axis=1))
                    small = short_nt(w_ref[2 * rows :, :], jnp.concatenate([high, low], axis=1))
                    approx = big[:rows] + (big[rows:] + small)
                    full = blocks[4 * kc + kx][:, ky * thin : (ky + 1) * thin]
                    e_out[:, block] = (full - approx).astype(jnp.bfloat16)
                    core = at[0] if kc == 0 else 1 - at[0]
                    place = (core * 4 + (at[1] + kx) % 4) * 4 + (at[2] + ky) % 4
                    place = pl.ds(pl.multiple_of(place * thin, thin), thin)
                    m_next = 0.9 * m[:, place] + 0.1 * approx
                    v_next = 0.95 * v[:, place] + 0.05 * approx * approx
                    m_out[:, block] = m_next
                    v_out[:, block] = v_next
                    root = v_next * fix_two
                    root = root * lax.rsqrt(root)
                    u_out[:, block] = ((m_next * fix_one) / (root + 1e-08)).astype(jnp.bfloat16)

        if extra:
            inv = refs[count + 11 + tail - 1]
            near = refs[count + 11 + 4 : count + 11 + tail - 1]
            for i, t in enumerate((*near, *refs[:count])):
                core = at[0] if i % 2 == 0 else 1 - at[0]
                owner = core * 4 + (at[1] + 4 - ORDER[i // 2]) % 4

                @pl.when(jnp.logical_and(pl.program_id(0) == 0, owner == at[3]))
                def _(t=t):
                    for j in range(4):
                        part = pl.ds(pl.multiple_of(((at[2] + 4 - j) % 4) * thin, thin), thin)
                        value = dot_nt(t[j * thin : (j + 1) * thin, :], inv[...])
                        outs[4][part, :] = value * (1.0 / REPS)

    def column(i, at):
        kc, kx = i % 2, i // 2 + which
        core = at[0] + kc - 2 * at[0] * kc
        return (0, core * 4 + (at[1] + 4 - kx) % 4)

    block = pl.BlockSpec((rows, wide), column)
    ins = [vmem()] * (count + 11)
    args = [place, *ts, *merged, weight, moment, second]
    specs = [block] * 4
    shapes = [
        jax.ShapeDtypeStruct((rows, cols), d) for d in (jnp.bfloat16, F32, F32, jnp.bfloat16)
    ]
    alias = {len(args) + i: i for i in range(len(before))}
    ins += [pl.BlockSpec(memory_space=pl.ANY)] * len(before) + [vmem()] * len(extra)
    args += [*before, *extra]
    if extra:
        specs.append(vmem())
        shapes.append(jax.ShapeDtypeStruct((wide, rank), F32))
    return pl.pallas_call(
        body,
        grid_spec=pltpu.PrefetchScalarGridSpec(
            num_scalar_prefetch=1, grid=(count,), in_specs=ins, out_specs=specs
        ),
        out_shape=shapes,
        input_output_aliases=alias,
        compiler_params=params(28),
        name="finish",
    )(*args)


def shift(value, axis, step):
    n = lax.axis_size(axis)
    return lax.ppermute(value, axis, [(i, (i + step) % n) for i in range(n)])


def device(y, x, core, z):
    return ((y * 4 + x) * 2 + core) * 8 + z


def spread(block, steps, held):
    pairs = []
    for y in range(4):
        for x in range(4):
            for core in range(2):
                for h in held:
                    z = (core * 4 + x + h) % 8
                    pairs.append((device(y, x, core, z), device(y, x, core, (z + steps) % 8)))
    return lax.ppermute(block, ALL, pairs)


def on_device(grads, errors, q_prev, moment, second):
    y, x, core, z = (lax.axis_index(a) for a in ALL)
    place = jnp.stack([core, x, y, z]).astype(jnp.int32)
    grads, errors = grads[0], errors[0]

    theirs = merge_half(place, True, grads, errors)
    came = {k: shift(theirs[k], "core", 1) for k in (1, 2, 3, 0)}
    mine = merge_half(place, False, grads, errors)
    merged = [*mine, *theirs]

    right = rows_of(place, q_prev)
    held = [0]
    for step in (4, 2, 1):
        new = [h + step for h in held]
        right = choose(place, new, spread(right, step, held), right)
        held = held + new

    parts = [shift(total([mine[k], came[k]]), "x", k) for k in (1, 2, 3)]
    blocks = sum_split([mine[0], came[0], *parts])
    m, p = left_part([blocks[0]] + [shift(blocks[k], "y", k) for k in (1, 2, 3)], right)

    for axis in ("x", "y"):
        p = total([p] + [shift(p, axis, k) for k in (1, 2, 3)])
    p = total([p, shift(p, "core", 1)])

    whole = lax.all_to_all(products(m, p), "z", 0, 0)
    whole = lax.all_to_all(sum_copies(whole), "z", 0, 0)
    t, gram = unpack(whole, m.shape[1] // 8)
    t = stack([t] + [shift(t, "y", k) for k in (1, 2, 3)])
    t, gram = lax.optimization_barrier((t, gram))
    def pair(block):
        return [block, shift(block, "core", 1)]

    near = pair(t)
    one, three = shift(t, "x", 1), shift(t, "x", 3)
    inverse, weight = invert(gram, p)
    out = finish(place, 0, near, weight, merged, moment, second)
    out, one, three = lax.optimization_barrier((out, one, three))

    upper, lower = halves(one, three)
    two = [shift(upper, "x", 1), shift(lower, "x", 3)]
    one, three = pair(one), pair(three)
    out = finish(place, 1, one, weight, merged, moment, second, out)
    out = finish(place, 3, three, weight, merged, moment, second, out)
    out, two = lax.optimization_barrier((out, two))
    two = pair(stack(two))
    e_next, m_next, v_next, update, q_next = finish(
        place, 2, two, weight, merged, moment, second, out, [*near, *one, *three, inverse]
    )
    return (e_next[None], q_next, m_next, v_next, update)


def solution(mesh):
    grid = Mesh(mesh.devices.reshape(4, 4, 2, 8), ALL)
    rep = ("y", "x", "core")
    return jax.shard_map(
        on_device,
        mesh=grid,
        in_specs=(P(rep, "z", None), P(rep, "z", None), P("z", None), P("z", None), P("z", None)),
        out_specs=(P(rep, "z", None), P("z", None), P("z", None), P("z", None), P("z", None)),
        check_vma=False,
    )
```

```python
import functools

import jax
import jax.numpy as jnp
from jax import lax
from jax.experimental import pallas as pl
from jax.experimental.pallas import tpu as pltpu
from jax.sharding import Mesh, PartitionSpec as P

ADAM_STEP = 10
HI = lax.Precision.HIGHEST
F32 = jnp.float32
ALL = ("y", "x", "core", "z")
REPS = 32


def vmem():
    return pl.BlockSpec(memory_space=pltpu.VMEM)


def params(mib=16):
    return pltpu.CompilerParams(vmem_limit_bytes=mib * 1024 * 1024)


def split(value):
    high = value.astype(jnp.bfloat16)
    rest = value - high.astype(F32)
    middle = rest.astype(jnp.bfloat16)
    return high, middle, (rest - middle.astype(F32)).astype(jnp.bfloat16)


def short_nt(a, b):
    return lax.dot_general(a, b, (((1,), (1,)), ((), ())), preferred_element_type=F32)


def dot_nt(a, b):
    return lax.dot_general(a, b, (((1,), (1,)), ((), ())), precision=HI, preferred_element_type=F32)


def merge_half(place, other, grads, errors):
    rows, cols = grads.shape
    wide = cols // 8
    thin = wide // 4

    def body(at, g, e, *outs):
        core = 1 - at[0] if other else at[0]
        for k in range(4):
            for j in range(4):
                block = core * 16 + (at[1] + k) % 4 * 4 + (at[2] + j) % 4
                block = pl.ds(pl.multiple_of(block * thin, thin), thin)
                value = g[:, block].astype(F32) + e[:, block].astype(F32)
                outs[k][:, j * thin : (j + 1) * thin] = value

    return pl.pallas_call(
        body,
        in_specs=[pl.BlockSpec(memory_space=pltpu.SMEM)] + [vmem()] * 2,
        out_specs=[vmem()] * 4,
        out_shape=[jax.ShapeDtypeStruct((rows, wide), F32)] * 4,
        compiler_params=params(),
        name="merge_half",
    )(place, grads, errors)


def add_two(own, came):
    rows, wide = own.shape
    tall = rows // 2

    def body(a, b, up, down):
        up[...] = a[:tall] + b[:tall]
        down[...] = a[tall:] + b[tall:]

    return pl.pallas_call(
        body,
        in_specs=[vmem()] * 2,
        out_specs=[vmem()] * 2,
        out_shape=[jax.ShapeDtypeStruct((tall, wide), F32)] * 2,
        compiler_params=params(),
        name="add_two",
    )(own, came)


def add_half(own, came, part, side):
    rows, wide = own.shape
    tall = rows // 2

    def body(a, b, c, out):
        for i in range(2):
            half = slice(i * tall, (i + 1) * tall)
            value = a[half] + b[half]
            out[half, :] = value + c[...] if i == side else value

    return pl.pallas_call(
        body,
        in_specs=[vmem()] * 3,
        out_specs=vmem(),
        out_shape=jax.ShapeDtypeStruct((rows, wide), F32),
        compiler_params=params(),
        name="add_half",
    )(own, came, part)


def sum_split(parts):
    rows, wide = parts[0].shape
    thin = wide // 4
    count = len(parts)

    def body(*refs):
        for k in range(4):
            value = refs[0][:, k * thin : (k + 1) * thin]
            for ref in refs[1:count]:
                value = value + ref[:, k * thin : (k + 1) * thin]
            refs[count + k][...] = value

    return pl.pallas_call(
        body,
        in_specs=[vmem()] * count,
        out_specs=[vmem()] * 4,
        out_shape=[jax.ShapeDtypeStruct((rows, thin), F32)] * 4,
        compiler_params=params(),
        name="sum_split",
    )(*parts)


def left_part(parts, right):
    rows, cols = parts[0].shape

    def body(a, b, c, d, q, m_out, p_out):
        m_out[...] = (a[...] + b[...]) + (c[...] + d[...])
        p_out[...] = jnp.dot(m_out[...], q[...], precision=HI, preferred_element_type=F32)

    return pl.pallas_call(
        body,
        in_specs=[vmem()] * 5,
        out_specs=[vmem()] * 2,
        out_shape=[
            jax.ShapeDtypeStruct((rows, cols), F32),
            jax.ShapeDtypeStruct((rows, right.shape[1]), F32),
        ],
        compiler_params=params(),
        name="left_part",
    )(*parts, right)


def products(m, p):
    cols, rank = m.shape[1], p.shape[1]
    high, low = cols // 8, rank // 8

    def body(m_ref, p_ref, out):
        p_val = p_ref[...]
        t = jnp.dot(m_ref[...].T, p_val, precision=HI, preferred_element_type=F32)
        gram = jnp.dot(p_val.T, p_val, precision=HI, preferred_element_type=F32)
        out[:, :high, :] = t.reshape(8, high, rank)
        out[:, high:, :] = gram.reshape(8, low, rank)

    return pl.pallas_call(
        body,
        in_specs=[vmem()] * 2,
        out_specs=vmem(),
        out_shape=jax.ShapeDtypeStruct((8, high + low, rank), F32),
        compiler_params=params(),
        name="products",
    )(m, p)


def total(parts):
    def body(*refs):
        value = refs[0][...]
        for ref in refs[1:-1]:
            value = value + ref[...]
        refs[-1][...] = value

    return pl.pallas_call(
        body,
        in_specs=[vmem()] * len(parts),
        out_specs=vmem(),
        out_shape=jax.ShapeDtypeStruct(parts[0].shape, F32),
        compiler_params=params(),
        name="total",
    )(*parts)


def stack(parts):
    rows, cols = parts[0].shape

    def body(*refs):
        for i in range(len(parts)):
            refs[-1][i * rows : (i + 1) * rows, :] = refs[i][...]

    return pl.pallas_call(
        body,
        in_specs=[vmem()] * len(parts),
        out_specs=vmem(),
        out_shape=jax.ShapeDtypeStruct((len(parts) * rows, cols), F32),
        compiler_params=params(),
        name="stack",
    )(*parts)


def halves(a, b):
    rows, cols = a.shape[0] // 2, a.shape[1]

    def body(a_ref, b_ref, up, down):
        up[...] = a_ref[:rows]
        down[...] = b_ref[rows:]

    return pl.pallas_call(
        body,
        in_specs=[vmem()] * 2,
        out_specs=[vmem()] * 2,
        out_shape=[jax.ShapeDtypeStruct((rows, cols), F32)] * 2,
        compiler_params=params(),
        name="halves",
    )(a, b)


def sum_copies(parts):
    def body(a, out):
        value = jnp.sum(a[...], axis=0)
        out[...] = jnp.broadcast_to(value[None], out.shape)

    return pl.pallas_call(
        body,
        in_specs=[vmem()],
        out_specs=vmem(),
        out_shape=jax.ShapeDtypeStruct(parts.shape, F32),
        compiler_params=params(),
        name="sum_copies",
    )(parts)


def unpack(whole, high):
    count, both, rank = whole.shape
    low = both - high

    def body(a, t, gram):
        for i in range(count):
            t[i * high : (i + 1) * high, :] = a[i, :high, :]
            gram[i * low : (i + 1) * low, :] = a[i, high:, :]

    return pl.pallas_call(
        body,
        in_specs=[vmem()],
        out_specs=[vmem()] * 2,
        out_shape=[
            jax.ShapeDtypeStruct((count * high, rank), F32),
            jax.ShapeDtypeStruct((count * low, rank), F32),
        ],
        compiler_params=params(),
        name="unpack",
    )(whole)


def rows_of(place, q_prev):
    rows = q_prev.shape[0] // 4

    def body(at, q, out):
        out[...] = q[pl.ds(pl.multiple_of(at[2] * rows, rows), rows), :]

    return pl.pallas_call(
        body,
        in_specs=[pl.BlockSpec(memory_space=pltpu.SMEM), vmem()],
        out_specs=vmem(),
        out_shape=jax.ShapeDtypeStruct((rows, q_prev.shape[1]), F32),
        compiler_params=params(),
        name="rows_of",
    )(place, q_prev)


def choose(place, hits, came, have, *after):
    def body(at, a, b, *refs):
        out = refs[-1]
        away = (at[3] + 8 - (at[0] * 4 + at[1])) % 8
        hit = functools.reduce(jnp.logical_or, [away == h for h in hits])
        out[...] = jnp.where(hit, a[...], b[...])

    return pl.pallas_call(
        body,
        in_specs=[pl.BlockSpec(memory_space=pltpu.SMEM)]
        + [vmem()] * 2
        + [pl.BlockSpec(memory_space=pl.ANY)] * len(after),
        out_specs=vmem(),
        out_shape=jax.ShapeDtypeStruct(came.shape, F32),
        compiler_params=params(),
        name="choose",
    )(place, came, have, *after)


ORDER = (0, 1, 3, 2)
UNIT = 8
STRIP = 16


def invert(gram, p):
    n = gram.shape[0]

    def unit(left, right, at):
        wide = (1, 2 * n)

        def element(i, j):
            return jnp.broadcast_to(left[i : i + 1, at + j : at + j + 1], wide)

        a = [[element(i, j) for j in range(i + 1)] for i in range(UNIT)]
        rows = [
            jnp.concatenate([left[i : i + 1, :], right[i : i + 1, :]], axis=1) for i in range(UNIT)
        ]
        for j in range(UNIT):
            scale = lax.rsqrt(a[j][j])
            rows[j] = rows[j] * scale
            col = [a[i][j] * scale for i in range(j + 1, UNIT)]
            for i in range(j + 1, UNIT):
                for k in range(j + 1, i + 1):
                    a[i][k] = a[i][k] - col[i - j - 1] * col[k - j - 1]
                rows[i] = rows[i] - col[i - j - 1] * rows[j]
        both = jnp.concatenate(rows, axis=0)
        return both[:, :n], both[:, n:]

    def body(g_ref, p_ref, inv_out, w_out, work):
        row = lax.broadcasted_iota(jnp.int32, (n, n), 0)
        col = lax.broadcasted_iota(jnp.int32, (n, n), 1)
        work[:, :n] = g_ref[...]
        work[:, n:] = jnp.where(row == col, 1.0, 0.0).astype(F32)
        for at in range(0, n, STRIP):
            mid, end = at + UNIT, at + STRIP
            left, right = unit(work[at:mid, :n], work[at:mid, n:], at)
            low_left, low_right = work[mid:end, :n], work[mid:end, n:]
            factors = left[:, mid:end].T
            for j in range(UNIT):
                factor = factors[:, j : j + 1]
                low_left = low_left - factor * left[j : j + 1, :]
                low_right = low_right - factor * right[j : j + 1, :]
            low_left, low_right = unit(low_left, low_right, mid)
            inv_out[at:mid, :] = right
            inv_out[mid:end, :] = low_right
            if end < n:
                strip = jnp.concatenate([left, low_left], axis=0)
                both = jnp.concatenate(
                    [strip, jnp.concatenate([right, low_right], axis=0)], axis=1
                )
                work[end:, :] -= lax.dot_general(
                    strip[:, end:],
                    both,
                    (((0,), (0,)), ((), ())),
                    precision=HI,
                    preferred_element_type=F32,
                )
        inv = inv_out[...]
        p_hat = dot_nt(p_ref[...], inv)
        weight = jnp.dot(p_hat, inv, precision=HI, preferred_element_type=F32) * (1.0 / REPS)
        high, middle, low = split(weight)
        for i, pair in enumerate(((high, high), (middle, middle), (low, high))):
            w_out[i * n : (i + 1) * n, :] = jnp.concatenate(pair, axis=1)

    return pl.pallas_call(
        body,
        in_specs=[vmem()] * 2,
        out_specs=[vmem()] * 2,
        out_shape=[jax.ShapeDtypeStruct((n, n), F32), jax.ShapeDtypeStruct((3 * n, 2 * n), jnp.bfloat16)],
        scratch_shapes=[pltpu.VMEM((n, 2 * n), F32)],
        compiler_params=params(),
        cost_estimate=pl.CostEstimate(flops=8 * 10**9, bytes_accessed=1 << 18, transcendentals=n),
        name="invert",
    )(gram, p)


def finish(place, which, ts, weight, merged, moment, second, before=(), extra=()):
    rows, cols = moment.shape
    count = len(ts)
    wide, rank = ts[0].shape
    thin = wide // 4
    fix_one = 1.0 / (1.0 - 0.9**ADAM_STEP)
    fix_two = 1.0 / (1.0 - 0.95**ADAM_STEP)
    tail = len(before) + len(extra)

    def body(at, *refs):
        blocks = refs[count : count + 8]
        w_ref, m, v = refs[count + 8 : count + 11]
        outs = refs[count + 11 + tail :]
        e_out, m_out, v_out, u_out = outs[:4]
        for i in range(count):

            @pl.when(pl.program_id(0) == i)
            def _(i=i):
                kc, kx = i % 2, (4 - i // 2 - which) % 4
                for j in range(4):
                    ky = (4 - j) % 4
                    block = pl.ds(pl.multiple_of(((at[2] + ky) % 4) * thin, thin), thin)
                    t = refs[i][j * thin : (j + 1) * thin, :]
                    high, middle, low = split(t)
                    big = short_nt(w_ref[: 2 * rows, :], jnp.concatenate([high, middle], axis=1))
                    small = short_nt(w_ref[2 * rows :, :], jnp.concatenate([high, low], axis=1))
                    approx = big[:rows] + (big[rows:] + small)
                    full = blocks[4 * kc + kx][:, ky * thin : (ky + 1) * thin]
                    e_out[:, block] = (full - approx).astype(jnp.bfloat16)
                    core = at[0] if kc == 0 else 1 - at[0]
                    place = (core * 4 + (at[1] + kx) % 4) * 4 + (at[2] + ky) % 4
                    place = pl.ds(pl.multiple_of(place * thin, thin), thin)
                    m_next = 0.9 * m[:, place] + 0.1 * approx
                    v_next = 0.95 * v[:, place] + 0.05 * approx * approx
                    m_out[:, block] = m_next
                    v_out[:, block] = v_next
                    root = v_next * fix_two
                    root = root * lax.rsqrt(root)
                    u_out[:, block] = ((m_next * fix_one) / (root + 1e-08)).astype(jnp.bfloat16)

        if extra:
            inv = refs[count + 11 + tail - 1]
            near = refs[count + 11 + 4 : count + 11 + tail - 1]
            for i, t in enumerate((*near, *refs[:count])):
                core = at[0] if i % 2 == 0 else 1 - at[0]
                owner = core * 4 + (at[1] + 4 - ORDER[i // 2]) % 4

                @pl.when(jnp.logical_and(pl.program_id(0) == 0, owner == at[3]))
                def _(t=t):
                    for j in range(4):
                        part = pl.ds(pl.multiple_of(((at[2] + 4 - j) % 4) * thin, thin), thin)
                        value = dot_nt(t[j * thin : (j + 1) * thin, :], inv[...])
                        outs[4][part, :] = value * (1.0 / REPS)

    def column(i, at):
        kc, kx = i % 2, i // 2 + which
        core = at[0] + kc - 2 * at[0] * kc
        return (0, core * 4 + (at[1] + 4 - kx) % 4)

    block = pl.BlockSpec((rows, wide), column)
    ins = [vmem()] * (count + 11)
    args = [place, *ts, *merged, weight, moment, second]
    specs = [block] * 4
    shapes = [
        jax.ShapeDtypeStruct((rows, cols), d) for d in (jnp.bfloat16, F32, F32, jnp.bfloat16)
    ]
    alias = {len(args) + i: i for i in range(len(before))}
    ins += [pl.BlockSpec(memory_space=pl.ANY)] * len(before) + [vmem()] * len(extra)
    args += [*before, *extra]
    if extra:
        specs.append(vmem())
        shapes.append(jax.ShapeDtypeStruct((wide, rank), F32))
    return pl.pallas_call(
        body,
        grid_spec=pltpu.PrefetchScalarGridSpec(
            num_scalar_prefetch=1, grid=(count,), in_specs=ins, out_specs=specs
        ),
        out_shape=shapes,
        input_output_aliases=alias,
        compiler_params=params(28),
        name="finish",
    )(*args)


def shift(value, axis, step):
    n = lax.axis_size(axis)
    return lax.ppermute(value, axis, [(i, (i + step) % n) for i in range(n)])


def device(y, x, core, z):
    return ((y * 4 + x) * 2 + core) * 8 + z


def spread(block, steps, held):
    pairs = []
    for y in range(4):
        for x in range(4):
            for core in range(2):
                for h in held:
                    z = (core * 4 + x + h) % 8
                    pairs.append((device(y, x, core, z), device(y, x, core, (z + steps) % 8)))
    return lax.ppermute(block, ALL, pairs)


def on_device(grads, errors, q_prev, moment, second):
    y, x, core, z = (lax.axis_index(a) for a in ALL)
    place = jnp.stack([core, x, y, z]).astype(jnp.int32)
    grads, errors = grads[0], errors[0]

    theirs = merge_half(place, True, grads, errors)
    came = {k: shift(theirs[k], "core", 1) for k in (2, 1, 3, 0)}
    mine = merge_half(place, False, grads, errors)
    merged = [*mine, *theirs]

    right = rows_of(place, q_prev)
    right = choose(place, [4], spread(right, 4, [0]), right)
    second_step = spread(right, 2, [0, 4])

    upper, lower = add_two(mine[2], came[2])
    upper, lower = shift(upper, "x", 1), shift(lower, "x", 3)
    parts = [
        shift(add_half(mine[1], came[1], upper, 0), "x", 1),
        shift(add_half(mine[3], came[3], lower, 1), "x", 3),
    ]
    blocks = sum_split([mine[0], came[0], *parts])
    right = choose(place, [2, 6], second_step, right, blocks[0])
    right = choose(place, [1, 3, 5, 7], spread(right, 1, [0, 2, 4, 6]), right)
    m, p = left_part([blocks[0]] + [shift(blocks[k], "y", k) for k in (1, 2, 3)], right)

    for axis in ("x", "y"):
        p = total([p] + [shift(p, axis, k) for k in (1, 2, 3)])
    p = total([p, shift(p, "core", 1)])

    whole = lax.all_to_all(products(m, p), "z", 0, 0)
    whole = lax.all_to_all(sum_copies(whole), "z", 0, 0)
    t, gram = unpack(whole, m.shape[1] // 8)
    t = stack([t] + [shift(t, "y", k) for k in (1, 2, 3)])
    t, gram = lax.optimization_barrier((t, gram))
    def pair(block):
        return [block, shift(block, "core", 1)]

    near = pair(t)
    one, three = shift(t, "x", 1), shift(t, "x", 3)
    inverse, weight = invert(gram, p)
    out = finish(place, 0, near, weight, merged, moment, second)
    out, one, three = lax.optimization_barrier((out, one, three))

    upper, lower = halves(one, three)
    two = [shift(upper, "x", 1), shift(lower, "x", 3)]
    one, three = pair(one), pair(three)
    out = finish(place, 1, one, weight, merged, moment, second, out)
    out = finish(place, 3, three, weight, merged, moment, second, out)
    out, two = lax.optimization_barrier((out, two))
    two = pair(stack(two))
    e_next, m_next, v_next, update, q_next = finish(
        place, 2, two, weight, merged, moment, second, out, [*near, *one, *three, inverse]
    )
    return (e_next[None], q_next, m_next, v_next, update)


def solution(mesh):
    grid = Mesh(mesh.devices.reshape(4, 4, 2, 8), ALL)
    rep = ("y", "x", "core")
    return jax.shard_map(
        on_device,
        mesh=grid,
        in_specs=(P(rep, "z", None), P(rep, "z", None), P("z", None), P("z", None), P("z", None)),
        out_specs=(P(rep, "z", None), P("z", None), P("z", None), P("z", None), P("z", None)),
        check_vma=False,
    )
```
